256 devices in a mesh: dp: 16 (over z, core), owner: 16 (over x, y).
Axes of the slice: x: 4, y: 4, z: 8, core: 2. Of those that a mesh axis runs over, the one named last changes fastest.
Arguments:
- partials: bfloat16 [16, 128, 512, 512], P('dp', None, 'owner'), may hold values from -0.25 to 0.25
- l_factor: float32 [256, 512, 512], P(('dp', 'owner')), as said below
- r_factor: float32 [256, 512, 512], P(('dp', 'owner')), as said below
- l_root: bfloat16 [256, 512, 512], P(('dp', 'owner')), as said below
- r_root: bfloat16 [256, 512, 512], P(('dp', 'owner')), as said below
- owner_table: int32 [16, 8], replicated, may hold values from 0 to 15, as said below
Outputs:
- preconditioned: bfloat16 [128, 512, 512], P('dp', 'owner')
- new_l_factor: float32 [256, 512, 512], P(('dp', 'owner'))
- new_r_factor: float32 [256, 512, 512], P(('dp', 'owner'))
- new_l_root: bfloat16 [256, 512, 512], P(('dp', 'owner'))
- new_r_root: bfloat16 [256, 512, 512], P(('dp', 'owner'))
The draws below stay inside these ranges and needn't reach their ends.
Inputs may be any that keep to these rules, and one draw needn't show every extreme that they name: `owner_table`: each row names 8 different owner indices. `l_factor`: symmetric positive definite. `r_factor`: symmetric positive definite. `l_root`: Symmetric. `r_root`: Symmetric.
All inputs are finite; a program needn't handle non-finite values.
Results may differ from the reference program's by a relative error of at most 0.04.
Values may be sent and summed in bfloat16 or wider, within the bound.
No kernel may reach another device: no remote copies, remote signals or barrier semaphores. Data moves between devices by JAX's collectives and lax.ppermute only.
A program may use at most 128 MiB of HBM per device.

```python
import math
import jax
import jax.numpy as jnp
from jax import lax

BLK = 512
NEWTON = 2
BROW = 8
NB = 128
SLOTS = 256
N_DP = 16
N_OWNER = 16


def cosine_table():
    rows = jnp.arange(BLK, dtype=jnp.float32)
    columns = jnp.arange(BLK, dtype=jnp.float32)
    angles = math.pi * (rows[:, None] + 0.5) * columns[None, :] / BLK
    weights = jnp.where(columns == 0.0, math.sqrt(1.0 / BLK), math.sqrt(2.0 / BLK)).astype(jnp.float32)
    return jnp.cos(angles) * weights[None, :]


def eigen_parts(key, salt, value_low, value_high, shift_low):
    key = jax.random.fold_in(key, salt)
    sign_rows_key, value_key, shift_key, sign_key = jax.random.split(key, 4)
    row_signs = jnp.where(jax.random.bernoulli(sign_rows_key, 0.5, (SLOTS, BLK, 1)), 1.0, -1.0).astype(jnp.float32)
    basis = row_signs * cosine_table()[None, :, :]
    log_values = jax.random.uniform(value_key, (SLOTS, BLK), jnp.float32, math.log(value_low), math.log(value_high))
    values = jnp.exp(log_values)
    magnitude = jax.random.uniform(shift_key, (SLOTS, BLK), jnp.float32, shift_low, 0.2)
    signs = jnp.where(jax.random.bernoulli(sign_key, 0.5, (SLOTS, BLK)), 1.0, -1.0).astype(jnp.float32)
    return (basis, values, signs * magnitude)


def compose(basis, spectrum):
    scaled = basis * spectrum[:, None, :]
    whole = jnp.einsum('sij,skj->sik', scaled, basis, precision=lax.Precision.HIGHEST)
    return 0.5 * (whole + jnp.swapaxes(whole, 1, 2))


def draw_l_factor(key, part):
    basis, values, shifts = eigen_parts(key, 101, 0.5, 10.0, 0.0)
    return compose(basis, values)


def draw_r_factor(key, part):
    basis, values, shifts = eigen_parts(key, 102, 0.5, 10.0, 0.0)
    return compose(basis, values)


def draw_l_root(key, part):
    basis, values, shifts = eigen_parts(key, 101, 0.5, 10.0, 0.0)
    return compose(basis, values ** (-0.25) * (1.0 + shifts)).astype(jnp.bfloat16)


def draw_r_root(key, part):
    basis, values, shifts = eigen_parts(key, 102, 0.5, 10.0, 0.0)
    return compose(basis, values ** (-0.25) * (1.0 + shifts)).astype(jnp.bfloat16)


def draw_owner_table(key, part):
    key = jax.random.fold_in(key, 5)
    row_keys = jax.random.split(key, N_DP)
    orders = jax.vmap(lambda row_key: jax.random.permutation(row_key, N_OWNER))(row_keys).astype(jnp.int32)
    first_row = orders[0]
    positions = jnp.arange(N_OWNER, dtype=jnp.int32)
    priority = jnp.where((first_row == 0) | (first_row == N_OWNER - 1), 0, 1).astype(jnp.int32) * N_OWNER + positions
    moved = first_row[jnp.argsort(priority)]
    orders = orders.at[0].set(moved)
    return orders[:, :BROW].astype(jnp.int32)


def raised(values, stream_key, source, target, parts, factor):
    owner, partner = [(jnp.arange(values.shape[dim]) // (values.shape[dim] // parts)).reshape([-1 if axis == dim else 1 for axis in range(values.ndim)]) for dim in (source, target)]
    chosen = jax.random.permutation(stream_key, parts)[partner]
    strong = (owner == chosen) | (owner == (partner + parts // 2) % parts)
    return jnp.where(strong, factor * values, values)


def levels(own_key, shape, cuts, least, high):
    gain, own = 1.0, jax.random.fold_in(own_key, 6)
    for dim, parts in cuts:
        draws = jnp.exp(jax.random.uniform(jax.random.fold_in(own, dim), (parts,), jnp.float32, least / len(cuts), high / len(cuts)))
        gain = gain * jnp.repeat(draws, shape[dim] // parts).reshape([-1 if axis == dim else 1 for axis in range(len(shape))])
    return gain


def gaussian_with(key, dims, width, most, cuts, heavy, kind=jnp.bfloat16):
    drawn = width * jax.random.normal(key, dims, jnp.float32)
    if cuts:
        drawn = drawn * levels(key, dims, cuts, -0.22, 0.18)
    return jnp.clip(raised(drawn, jax.random.fold_in(key, 3), *heavy), -most, most).astype(kind)


def setup_inputs(seed: int = 0) -> dict:
    key_of = jax.random.split(jax.random.key(seed), 7)
    return {
        "partials": gaussian_with(key_of[0], (N_DP, NB, BLK, BLK), (BLK * (N_DP + 6) // 10) ** -0.5, 0.25, ((0, 16), (2, 16)), (0, 1, 16, 2.0)),
        "l_factor": draw_l_factor(jax.random.fold_in(key_of[6], 71), 0),
        "r_factor": draw_r_factor(jax.random.fold_in(key_of[6], 71), 0),
        "l_root": draw_l_root(jax.random.fold_in(key_of[6], 71), 0),
        "r_root": draw_r_root(jax.random.fold_in(key_of[6], 71), 0),
        "owner_table": draw_owner_table(jax.random.fold_in(key_of[6], 71), 0),
    }


BETA = 0.9


def matmul_high(left, right):
    return jnp.dot(left, right, precision=lax.Precision.HIGHEST, preferred_element_type=jnp.float32)


def inverse_root(factor, root):
    identity = jnp.eye(factor.shape[0], dtype=jnp.float32)
    current = root.astype(jnp.float32)
    square = matmul_high(current, current)
    fourth = matmul_high(square, square)
    product = matmul_high(fourth, factor)
    for newton_turn in range(NEWTON):
        step_matrix = (5.0 * identity - product) * 0.25
        current = matmul_high(current, step_matrix)
        if newton_turn + 1 < NEWTON:
            step_square = matmul_high(step_matrix, step_matrix)
            step_fourth = matmul_high(step_square, step_square)
            product = matmul_high(step_fourth, product)
    return current.astype(jnp.bfloat16)


def update_block(gradient, l_old, r_old, l_inv, r_inv):
    left_gram = jnp.dot(gradient, gradient.T, preferred_element_type=jnp.float32)
    right_gram = jnp.dot(gradient.T, gradient, preferred_element_type=jnp.float32)
    l_new = BETA * l_old + (1.0 - BETA) * left_gram
    r_new = BETA * r_old + (1.0 - BETA) * right_gram
    left_applied = jnp.dot(l_inv, gradient, preferred_element_type=jnp.float32).astype(jnp.bfloat16)
    precond = jnp.dot(left_applied, r_inv, preferred_element_type=jnp.float32).astype(jnp.bfloat16)
    return l_new, r_new, inverse_root(l_new, l_inv), inverse_root(r_new, r_inv), precond


def reference(partials, l_factor, r_factor, l_root, r_root, owner_table):
    def one_block(block_index):
        group_of = block_index // BROW
        position = block_index % BROW
        owner_of = owner_table[group_of, position]
        slot_index = (group_of * N_OWNER + owner_of).astype(jnp.int32)
        replicas = lax.dynamic_index_in_dim(partials, block_index, 1, keepdims=False)
        gradient = jnp.sum(replicas.astype(jnp.float32), axis=0).astype(jnp.bfloat16)
        l_old = lax.dynamic_index_in_dim(l_factor, slot_index, 0, keepdims=False)
        r_old = lax.dynamic_index_in_dim(r_factor, slot_index, 0, keepdims=False)
        l_inv = lax.dynamic_index_in_dim(l_root, slot_index, 0, keepdims=False)
        r_inv = lax.dynamic_index_in_dim(r_root, slot_index, 0, keepdims=False)
        l_new, r_new, l_next, r_next, precond = update_block(gradient, l_old, r_old, l_inv, r_inv)
        return l_new, r_new, l_next, r_next, precond, slot_index

    results = lax.map(one_block, jnp.arange(NB, dtype=jnp.int32))
    slot_list = results[5]
    new_l_factor = l_factor.at[slot_list].set(results[0])
    new_r_factor = r_factor.at[slot_list].set(results[1])
    new_l_root = l_root.at[slot_list].set(results[2])
    new_r_root = r_root.at[slot_list].set(results[3])
    return results[4], new_l_factor, new_r_factor, new_l_root, new_r_root
```

```python
import jax
import jax.numpy as jnp
from jax import lax
from jax.sharding import PartitionSpec as P

BETA = 0.9
HIGH = lax.Precision.HIGH
F32 = jnp.float32
BF16 = jnp.bfloat16


def dot(left, right, precision=None):
    return jnp.dot(left, right, precision=precision, preferred_element_type=F32)


def add(left, right):
    return (left.astype(F32) + right.astype(F32)).astype(BF16)


def ring_sum(local, dp_size):
    chips = dp_size // 2
    half = chips // 2
    me = lax.axis_index("dp")
    z, core = me // 2, me % 2
    groups = local.shape[0] // dp_size
    grouped = local.reshape(chips, 2, groups, *local.shape[1:])
    sibling = [(i, i ^ 1) for i in range(dp_size)]
    right = [(i, (i + 2) % dp_size) for i in range(dp_size)]
    left = [(i, (i - 2) % dp_size) for i in range(dp_size)]

    def chunk(distance, which):
        start = (lax.rem(z + distance + chips, chips), which) + (0,) * (grouped.ndim - 2)
        return lax.dynamic_slice(grouped, start, (1, 1) + grouped.shape[2:])[0, 0]

    paired = {}
    for distance in range(half, -1, -1):
        offsets = [distance] if distance in (0, half) else [distance, -distance]
        away = jnp.stack([chunk(d, 1 - core) for d in offsets])
        came = lax.ppermute(away, "dp", sibling)
        for k, d in enumerate(offsets):
            paired[d] = add(chunk(d, core), came[k])
    cut = groups // 2
    from_left = lax.ppermute(paired[half][:cut], "dp", right)
    from_right = lax.ppermute(paired[half][cut:], "dp", left)
    for distance in range(half - 1, 0, -1):
        go_right, go_left = paired[distance], paired[-distance]
        if distance == half - 1:
            go_right = jnp.concatenate([add(go_right[:cut], from_left), go_right[cut:]])
            go_left = jnp.concatenate([go_left[:cut], add(go_left[cut:], from_right)])
        else:
            go_right, go_left = add(go_right, from_left), add(go_left, from_right)
        from_left = lax.ppermute(go_right, "dp", right)
        from_right = lax.ppermute(go_left, "dp", left)
    total = paired[0].astype(F32) + from_left.astype(F32) + from_right.astype(F32)
    return total.astype(BF16)


def prepare(factor, root):
    square = dot(root, root)
    fourth = dot(square, square, HIGH)
    return fourth, BETA * dot(fourth, factor, HIGH)


def refresh(fourth, product, gram, root):
    product = product + dot(fourth, gram, HIGH)
    order = product.shape[0]
    identity = jnp.eye(order, dtype=F32)
    e1 = 0.25 * (identity - product)
    e2 = dot(e1, e1, HIGH)
    inner = dot(e2, 4.75 * e1 + e2, HIGH)
    correction = e1 + dot(e2, 2.5 * identity + 7.5 * e1 + 8.75 * e2 + inner, HIGH)
    return root.astype(F32) + dot(root, correction.astype(BF16))


def body(partials, l_factor, r_factor, l_root, r_root, owner_table):
    owners = lax.axis_size("owner")
    dp_size = lax.axis_size("dp")
    group_index = lax.axis_index("dp")
    owner_index = lax.axis_index("owner")
    my_row = lax.dynamic_index_in_dim(owner_table, group_index, 0, keepdims=False)
    slice_rows, row_width = partials.shape[2:]
    row_blocks = my_row.shape[0]
    owner_ids = jnp.arange(owners, dtype=jnp.int32)
    l_old, r_old, l_inv, r_inv = l_factor[0], r_factor[0], l_root[0], r_root[0]
    l_fourth, l_product = prepare(l_old, l_inv)
    r_fourth, r_product = prepare(r_old, r_inv)
    summed = ring_sum(partials[0], dp_size)
    select = owner_ids[:, None] == my_row[None, :]
    outgoing = jnp.sum(
        jnp.where(select[:, :, None, None], summed[None], jnp.zeros((), BF16)), axis=1, dtype=BF16
    )
    arrived = lax.all_to_all(outgoing, "owner", split_axis=0, concat_axis=0, tiled=True)
    gradient = arrived.reshape(owners * slice_rows, row_width)
    is_owner = jnp.any(my_row == owner_index)
    left_applied = dot(l_inv, gradient).astype(BF16)
    precond = dot(left_applied, r_inv).astype(BF16)
    returned = lax.all_to_all(
        precond.reshape(owners, slice_rows, row_width),
        "owner",
        split_axis=0,
        concat_axis=0,
        tiled=True,
    )
    my_blocks = jnp.take(returned, my_row, axis=0, mode="clip")
    l_gram = (1.0 - BETA) * dot(gradient, gradient.T)
    r_gram = (1.0 - BETA) * dot(gradient.T, gradient)
    l_new = BETA * l_old + l_gram
    r_new = BETA * r_old + r_gram
    l_next = refresh(l_fourth, l_product, l_gram, l_inv).astype(BF16)
    r_next = refresh(r_fourth, r_product, r_gram, r_inv).astype(BF16)
    l_out = jnp.where(is_owner, l_new, l_old)[None]
    r_out = jnp.where(is_owner, r_new, r_old)[None]
    l_root_out = jnp.where(is_owner, l_next, l_inv)[None]
    r_root_out = jnp.where(is_owner, r_next, r_inv)[None]
    return (my_blocks, l_out, r_out, l_root_out, r_root_out)


def solution(mesh):
    placed = (
        P("dp", None, "owner", None),
        P(("dp", "owner"), None, None),
        P(("dp", "owner"), None, None),
        P(("dp", "owner"), None, None),
        P(("dp", "owner"), None, None),
        P(),
    )
    return jax.shard_map(
        body,
        mesh=mesh,
        in_specs=placed,
        out_specs=(
            P("dp", "owner", None),
            P(("dp", "owner"), None, None),
            P(("dp", "owner"), None, None),
            P(("dp", "owner"), None, None),
            P(("dp", "owner"), None, None),
        ),
        check_vma=False,
    )
```
